32 devices in a mesh: parts: 2 (over y), outer: 4 (over x, core), blk: 4 (over z).
Axes of the slice: x: 2, y: 2, z: 4, core: 2. Of those that a mesh axis runs over, the one named last changes fastest.
Arguments:
- q_teacher: bfloat16 [4096, 512], P(('parts', 'outer', 'blk')), parts along dimension 0, may hold values from -30 to 30
- k_teacher: bfloat16 [4096, 512], P(('parts', 'outer', 'blk')), parts along dimension 0, may hold values from -30 to 30
- q_student: bfloat16 [4096, 512], P(('parts', 'outer', 'blk')), parts along dimension 0, may hold values from -30 to 30
- k_student: bfloat16 [4096, 512], P(('parts', 'outer', 'blk')), parts along dimension 0, may hold values from -30 to 30
- positions: int32 [4096], P(('parts', 'outer', 'blk')), parts along dimension 0, may hold values from 0 to 511, as said below
Outputs:
- grad_query: float32 [4096, 512], P(('parts', 'outer', 'blk')), parts along dimension 0
- grad_key: float32 [4096, 512], P(('parts', 'outer', 'blk')), parts along dimension 0
The draws below stay inside these ranges and needn't reach their ends.
There are 2 independent parts, one for each index of `parts`. The reference program is written for one: setup_inputs(seed, part) draws one part's arguments, and reference() takes and returns one part's arrays. A program takes and returns all parts, laid end to end along the dimension named above; each array names one. Nothing has to cross between parts.
Inputs may be any that keep to these rules, and one draw needn't show every extreme that they name: `positions`: positions count 0, 1, 2, ... from the first token of each document; documents are 64 to 512 tokens long (the last may be cut by the sequence's end) and one is exactly 512 long.
All inputs are finite; a program needn't handle non-finite values.
Results may differ from the reference program's by a relative error of at most 0.0085.
Values may be sent and summed in bfloat16 or wider, within the bound.
A program may use at most 64 MiB of HBM per device.

```python
import jax
import jax.numpy as jnp
from jax import lax

HEADS = 4
HEAD_DIM = 128
LOSS_SCALE = 256
DOC_MAX = 512
TOKENS = 2048


def drawn_pair(key, label_number):
    folded = jax.random.fold_in(key, label_number)
    key_query, key_keys = jax.random.split(folded, 2)
    extent = (TOKENS, HEADS * HEAD_DIM)
    queries = jnp.clip(jax.random.normal(key_query, extent, jnp.float32), -5.0, 5.0)
    keyset = jnp.clip(jax.random.normal(key_keys, extent, jnp.float32), -5.0, 5.0)
    return (queries, keyset)


def draw_q_teacher(key, part):
    return drawn_pair(key, 11)[0].astype(jnp.bfloat16)


def draw_k_teacher(key, part):
    return drawn_pair(key, 11)[1].astype(jnp.bfloat16)


def draw_q_student(key, part):
    return drawn_pair(key, 23)[0].astype(jnp.bfloat16)


def draw_k_student(key, part):
    return drawn_pair(key, 23)[1].astype(jnp.bfloat16)


def draw_positions(key, part):
    key_length, key_choice = jax.random.split(jax.random.fold_in(key, 7))
    doc_count = TOKENS // (DOC_MAX // 8) + 2
    lengths = jax.random.randint(key_length, (doc_count,), DOC_MAX // 8, DOC_MAX + 1)
    picked = jax.random.randint(key_choice, (), 0, 2)
    lengths = jnp.where(jnp.arange(doc_count) == picked, DOC_MAX, lengths)
    starts = jnp.cumsum(lengths) - lengths
    token_index = jnp.arange(TOKENS, dtype=jnp.int32)
    owner = jnp.searchsorted(starts, token_index, side='right') - 1
    return (token_index - starts[owner]).astype(jnp.int32)


def setup_inputs(seed: int = 0, part: int = 0) -> dict:
    splits = jax.random.split(jax.random.key(seed), 6)
    part_keys = jax.random.split(jax.random.fold_in(splits[5], part), 6)
    return {
        "q_teacher": draw_q_teacher(jax.random.fold_in(jax.random.fold_in(splits[5], part), 71), part),
        "k_teacher": draw_k_teacher(jax.random.fold_in(jax.random.fold_in(splits[5], part), 71), part),
        "q_student": draw_q_student(jax.random.fold_in(jax.random.fold_in(splits[5], part), 71), part),
        "k_student": draw_k_student(jax.random.fold_in(jax.random.fold_in(splits[5], part), 71), part),
        "positions": draw_positions(jax.random.fold_in(jax.random.fold_in(splits[5], part), 71), part),
    }


def heads_view(matrix):
    return matrix.reshape(matrix.shape[0], HEADS, HEAD_DIM).astype(jnp.float32)


def round_half(values):
    return lax.optimization_barrier(values.astype(jnp.bfloat16)).astype(jnp.float32)


def probabilities(scores, is_seen):
    masked = jnp.where(is_seen[None], scores, -jnp.inf)
    top_score = jnp.max(masked, axis=2, keepdims=True)
    total_sum = jnp.sum(jnp.where(is_seen[None], jnp.exp(scores - top_score), 0.0), axis=2, keepdims=True)
    log_total = top_score + jnp.log(total_sum)
    return jnp.where(is_seen[None], jnp.exp(scores - log_total), 0.0)


def reference(q_teacher, k_teacher, q_student, k_student, positions):
    group_len = DOC_MAX
    group_count = TOKENS // group_len
    inv_root = HEAD_DIM ** -0.5
    highest = lax.Precision.HIGHEST
    filler = jnp.zeros((group_len, HEADS * HEAD_DIM), jnp.bfloat16)
    teacher_keys = heads_view(jnp.concatenate([filler, k_teacher], 0))
    student_keys = heads_view(jnp.concatenate([filler, k_student], 0))
    teacher_queries = heads_view(q_teacher)
    student_queries = heads_view(q_student)
    token_index = jnp.arange(TOKENS, dtype=jnp.int32)
    doc_start = token_index - positions

    def one_group(group_id):
        first_row = (group_id * group_len).astype(jnp.int32)
        query_rows = first_row + jnp.arange(group_len, dtype=jnp.int32)
        key_rows = first_row - group_len + jnp.arange(2 * group_len, dtype=jnp.int32)
        query_low = lax.dynamic_slice_in_dim(doc_start, first_row, group_len, 0)
        is_seen = (key_rows[None, :] <= query_rows[:, None]) & (key_rows[None, :] >= query_low[:, None])
        teacher_block = lax.dynamic_slice_in_dim(teacher_queries, first_row, group_len, 0)
        student_block = lax.dynamic_slice_in_dim(student_queries, first_row, group_len, 0)
        teacher_near = lax.dynamic_slice_in_dim(teacher_keys, first_row, 2 * group_len, 0)
        student_near = lax.dynamic_slice_in_dim(student_keys, first_row, 2 * group_len, 0)
        teacher_scores = jnp.einsum("qhd,khd->hqk", teacher_block, teacher_near, precision=highest) * inv_root
        student_scores = jnp.einsum("qhd,khd->hqk", student_block, student_near, precision=highest) * inv_root
        teacher_prob = probabilities(teacher_scores, is_seen)
        student_prob = probabilities(student_scores, is_seen)
        teacher_weight = round_half(teacher_prob)
        student_weight = round_half(student_prob)
        student_sum = jnp.einsum("hqk,khd->qhd", student_weight, student_near, precision=highest)
        teacher_sum = jnp.einsum("hqk,khd->qhd", teacher_weight, student_near, precision=highest)
        grad_query = LOSS_SCALE * inv_root * (student_sum - teacher_sum)
        score_grad = round_half(LOSS_SCALE * (student_prob - teacher_prob))
        grad_keys = inv_root * jnp.einsum("hqk,qhd->khd", score_grad, student_block, precision=highest)
        return grad_query, grad_keys[:group_len], grad_keys[group_len:]

    grad_query, grad_prev, grad_own = lax.map(one_group, jnp.arange(group_count, dtype=jnp.int32))
    shifted = jnp.concatenate([grad_prev[1:], jnp.zeros_like(grad_prev[:1])], 0)
    grad_key = grad_own + shifted
    return grad_query.reshape(TOKENS, HEADS * HEAD_DIM), grad_key.reshape(TOKENS, HEADS * HEAD_DIM)
```

```python
import functools
import math

import jax
import jax.numpy as jnp
from jax import lax
from jax.experimental import pallas as pl
from jax.experimental.pallas import tpu as pltpu
from jax.sharding import PartitionSpec as P

HEADS = 4
HEAD_DIM = 128
LOSS_SCALE = 256
LOWEST = -1e30
INV_ROOT = HEAD_DIM ** (-0.5)
MESH = pl.DeviceIdType.MESH


def kernel(
    blk, total, rows,
    qt_ref, kt_ref, qs_ref, ks_ref, pos_ref,
    dq_ref, dk_ref,
    ktb, ksb, qtb, qsb, posb,
    acc, dq_out, dq_in, dk_out, dk_in, part_out, part_in,
    local_sem, send_sem, recv_sem, fsend, frecv, psend, precv,
    dqs, dqr, dks, dkr,
):
    prior = blk // HEADS
    team_rows = HEADS * rows
    own = prior * team_rows
    window = own + rows
    o = lax.axis_index("outer")
    z = lax.axis_index("blk")
    line = o * blk + z
    r = lax.rem(z, HEADS)
    z0 = z - r

    def at(index):
        return {"outer": index // blk, "blk": lax.rem(index, blk)}

    def mate(place):
        return {"outer": o, "blk": z0 + place}

    barrier = pltpu.get_barrier_semaphore()
    for k in range(1, HEADS):
        pl.semaphore_signal(
            barrier, inc=1, device_id=mate(lax.rem(r + k, HEADS)), device_id_type=MESH
        )
    for p in range(1, prior + 1):
        @pl.when(line >= HEADS * p)
        def _():
            pl.semaphore_signal(
                barrier, inc=1, device_id=at(line - HEADS * p), device_id_type=MESH
            )

        @pl.when(line + HEADS * p < total)
        def _():
            pl.semaphore_signal(
                barrier, inc=1, device_id=at(line + HEADS * p), device_id_type=MESH
            )

    def slab(place):
        return pl.ds(pl.multiple_of(place * rows, rows), rows)

    def cols(place):
        return pl.ds(pl.multiple_of(place * HEAD_DIM, HEAD_DIM), HEAD_DIM)

    def own_slab(place):
        return pl.ds(pl.multiple_of(own + place * rows, rows), rows)

    def routes(head, place):
        return (
            (kt_ref.at[:, cols(head)], ktb.at[own_slab(place), :]),
            (ks_ref.at[:, cols(head)], ksb.at[own_slab(place), :]),
            (qt_ref.at[:, cols(head)], qtb.at[slab(place), :]),
            (qs_ref.at[:, cols(head)], qsb.at[slab(place), :]),
            (pos_ref, posb.at[place]),
        )

    locals_ = [
        pltpu.make_async_copy(src, dst, local_sem.at[a])
        for a, (src, dst) in enumerate(routes(r, r))
    ]
    for copy in locals_:
        copy.start()

    for p in range(1, prior + 1):
        @pl.when(line < HEADS * p)
        def _():
            lo = (prior - p) * team_rows
            ktb[lo : lo + team_rows, :] = jnp.zeros((team_rows, HEAD_DIM), jnp.bfloat16)
            ksb[lo : lo + team_rows, :] = jnp.zeros((team_rows, HEAD_DIM), jnp.bfloat16)

    before = jnp.minimum(line // HEADS, prior)
    after = jnp.minimum((total - 1 - line) // HEADS, prior)
    pl.semaphore_wait(barrier, HEADS - 1 + before + after)

    def outgoing(k, a):
        place = lax.rem(r + k, HEADS)
        src, dst = routes(place, r)[a]
        return pltpu.make_async_remote_copy(
            src_ref=src, dst_ref=dst, send_sem=send_sem.at[k - 1, a], recv_sem=recv_sem.at[r, a],
            device_id=mate(place), device_id_type=MESH,
        )

    def incoming(k, a):
        place = lax.rem(r + k, HEADS)
        src, dst = routes(r, place)[a]
        return pltpu.make_async_remote_copy(
            src_ref=src, dst_ref=dst, send_sem=send_sem.at[k - 1, a],
            recv_sem=recv_sem.at[place, a],
            device_id=mate(place), device_id_type=MESH,
        )

    for group in ((0, 1), (2, 3, 4)):
        for k in range(1, HEADS):
            for a in group:
                outgoing(k, a).start()

    def forward(p, k, a, target):
        place = lax.rem(r + k, HEADS)
        buf = (ktb, ksb)[a]
        there = pl.ds(
            pl.multiple_of((prior - p) * team_rows + place * rows, rows), rows
        )
        return pltpu.make_async_remote_copy(
            src_ref=buf.at[own_slab(place), :], dst_ref=buf.at[there, :],
            send_sem=fsend.at[p - 1, place, a], recv_sem=frecv.at[p - 1, place, a],
            device_id=at(target), device_id_type=MESH,
        )

    def forward_all(k):
        for p in range(1, prior + 1):
            @pl.when(line + HEADS * p < total)
            def _():
                for a in range(2):
                    forward(p, k, a, line + HEADS * p).start()

    locals_[0].wait()
    locals_[1].wait()
    forward_all(0)
    acc[...] = jnp.zeros_like(acc)
    for copy in locals_[2:]:
        copy.wait()
    for k in range(1, HEADS):
        incoming(k, 0).wait_recv()
        incoming(k, 1).wait_recv()
        forward_all(k)
    for k in range(1, HEADS):
        for a in (2, 3, 4):
            incoming(k, a).wait_recv()
    for p in range(1, prior + 1):
        @pl.when(line >= HEADS * p)
        def _():
            for k in range(HEADS):
                for a in range(2):
                    forward(p, k, a, line - HEADS * p).wait_recv()

    def send_part(block, target):
        p = prior - block // HEADS
        j = block % HEADS
        return pltpu.make_async_remote_copy(
            src_ref=part_out.at[block], dst_ref=part_in.at[p - 1, j],
            send_sem=psend.at[block], recv_sem=precv.at[p - 1, j],
            device_id=at(target), device_id_type=MESH,
        )

    def return_part(block):
        p = prior - block // HEADS

        @pl.when(line >= HEADS * p)
        def _():
            part_out[block] = acc[block * rows : (block + 1) * rows, :].astype(jnp.bfloat16)
            send_part(block, line - HEADS * p).start()

    def result(out, into, send, recv, place, head):
        return pltpu.make_async_remote_copy(
            src_ref=out.at[place], dst_ref=into.at[head],
            send_sem=send.at[place], recv_sem=recv.at[head],
            device_id=mate(place), device_id_type=MESH,
        )

    def give(i, value, ref, out, into, send, recv):
        @pl.when(r == i)
        def _():
            ref[:, cols(r)] = value

        @pl.when(r != i)
        def _():
            out[i] = value.astype(jnp.bfloat16)
            result(out, into, send, recv, i, r).start()

    ahead = lax.broadcasted_iota(jnp.int32, (window, rows), 0) - lax.broadcasted_iota(
        jnp.int32, (window, rows), 1
    ) - own
    power = INV_ROOT * math.log2(math.e)

    def weights(keys, queries, seen):
        scores = lax.dot_general(
            keys, queries, (((1,), (1,)), ((), ())), preferred_element_type=jnp.float32
        )
        masked = jnp.where(seen, scores, LOWEST)
        top = jnp.max(masked, axis=0, keepdims=True)
        raised = jnp.exp2((masked - top) * power)
        return raised, LOSS_SCALE / jnp.sum(raised, axis=0, keepdims=True)

    for i in range(HEADS):
        lo = i * rows
        seen = (ahead <= 0) & (ahead >= -posb[i])
        queries = qsb[lo : lo + rows, :]
        keys = ksb[lo : lo + window, :]
        t_raised, t_scale = weights(ktb[lo : lo + window, :], qtb[lo : lo + rows, :], seen)
        s_raised, s_scale = weights(keys, queries, seen)
        grad = (s_raised * s_scale - t_raised * t_scale).astype(jnp.bfloat16)
        acc[lo : lo + window, :] += jnp.dot(
            grad, queries, preferred_element_type=jnp.float32
        ) * INV_ROOT
        return_part(i)
        dq = lax.dot_general(
            grad, keys, (((0,), (0,)), ((), ())), preferred_element_type=jnp.float32
        ) * INV_ROOT
        give(i, dq, dq_ref, dq_out, dq_in, dqs, dqr)
    for block in range(HEADS, blk):
        return_part(block)

    for j in range(HEADS):
        for p in range(1, prior + 1):
            @pl.when(line + HEADS * p < total)
            def _():
                send_part((prior - p) * HEADS + j, line + HEADS * p).wait_recv()
                lo = own + j * rows
                acc[lo : lo + rows, :] += part_in[p - 1, j].astype(jnp.float32)
        give(
            j, acc[own + j * rows : own + (j + 1) * rows, :], dk_ref, dk_out, dk_in, dks, dkr
        )

    for ref, out, into, send, recv in (
        (dq_ref, dq_out, dq_in, dqs, dqr),
        (dk_ref, dk_out, dk_in, dks, dkr),
    ):
        for k in range(1, HEADS):
            place = lax.rem(r + k, HEADS)
            result(out, into, send, recv, place, place).wait_recv()
            ref[:, cols(place)] = into[place].astype(jnp.float32)

    for k in range(1, HEADS):
        for a in range(5):
            outgoing(k, a).wait_send()
        place = lax.rem(r + k, HEADS)
        result(dq_out, dq_in, dqs, dqr, place, r).wait_send()
        result(dk_out, dk_in, dks, dkr, place, r).wait_send()
    for p in range(1, prior + 1):
        @pl.when(line + HEADS * p < total)
        def _():
            for k in range(HEADS):
                for a in range(2):
                    forward(p, k, a, line + HEADS * p).wait_send()

        @pl.when(line >= HEADS * p)
        def _():
            for j in range(HEADS):
                send_part((prior - p) * HEADS + j, line - HEADS * p).wait_send()


def body(q_teacher, k_teacher, q_student, k_student, positions):
    rows, width = q_teacher.shape
    blk = lax.axis_size("blk")
    total = lax.axis_size("outer") * blk
    prior = blk // HEADS
    span = (blk + HEADS) * rows
    bf16, f32 = jnp.bfloat16, jnp.float32
    tile = (rows, HEAD_DIM)
    dma = pltpu.SemaphoreType.DMA
    pairs = HEADS * (span * rows) * HEAD_DIM
    return pl.pallas_call(
        functools.partial(kernel, blk, total, rows),
        out_shape=[jax.ShapeDtypeStruct((rows, width), f32)] * 2,
        in_specs=[pl.BlockSpec(memory_space=pl.ANY)] * 5,
        out_specs=[pl.BlockSpec(memory_space=pltpu.VMEM)] * 2,
        scratch_shapes=[
            pltpu.VMEM((span, HEAD_DIM), bf16),
            pltpu.VMEM((span, HEAD_DIM), bf16),
            pltpu.VMEM((HEADS * rows, HEAD_DIM), bf16),
            pltpu.VMEM((HEADS * rows, HEAD_DIM), bf16),
            pltpu.VMEM((HEADS, 1, rows), jnp.int32),
            pltpu.VMEM((span, HEAD_DIM), f32),
            pltpu.VMEM((HEADS,) + tile, bf16),
            pltpu.VMEM((HEADS,) + tile, bf16),
            pltpu.VMEM((HEADS,) + tile, bf16),
            pltpu.VMEM((HEADS,) + tile, bf16),
            pltpu.VMEM((blk,) + tile, bf16),
            pltpu.VMEM((prior, HEADS) + tile, bf16),
            dma((5,)),
            dma((HEADS - 1, 5)),
            dma((HEADS, 5)),
            dma((prior, HEADS, 2)),
            dma((prior, HEADS, 2)),
            dma((blk,)),
            dma((prior, HEADS)),
            dma((HEADS,)),
            dma((HEADS,)),
            dma((HEADS,)),
            dma((HEADS,)),
        ],
        compiler_params=pltpu.CompilerParams(
            collective_id=0, has_side_effects=True, vmem_limit_bytes=32 * 1024 * 1024
        ),
        cost_estimate=pl.CostEstimate(
            flops=8 * pairs, bytes_accessed=10 * rows * width * 2, transcendentals=2 * pairs // HEAD_DIM
        ),
    )(q_teacher, k_teacher, q_student, k_student, positions.reshape(1, rows))


def solution(mesh):
    spec = P(("parts", "outer", "blk"), None)
    return jax.shard_map(
        body,
        mesh=mesh,
        in_specs=(spec, spec, spec, spec, P(("parts", "outer", "blk"))),
        out_specs=(spec, spec),
        check_vma=False,
    )
```

```python
import functools
import math

import jax
import jax.numpy as jnp
from jax import lax
from jax.experimental import pallas as pl
from jax.experimental.pallas import tpu as pltpu
from jax.sharding import PartitionSpec as P

HEADS = 4
HEAD_DIM = 128
LOSS_SCALE = 256
LOWEST = -1e30
INV_ROOT = HEAD_DIM ** (-0.5)
MESH = pl.DeviceIdType.MESH
ORDER = (3, 2, 1)


def kernel(
    blk, total, rows,
    qt_ref, kt_ref, qs_ref, ks_ref, pos_ref,
    dq_ref, dk_ref,
    ktb, ksb, qtb, qsb, posb,
    teacher, acc, dq_out, dk_out, part_out, part_in,
    local_sem, send_sem, recv_sem, fsend, frecv, psend, precv,
    dqs, dqr, dks, dkr,
):
    prior = blk // HEADS
    team_rows = HEADS * rows
    own = prior * team_rows
    window = own + rows
    o = lax.axis_index("outer")
    z = lax.axis_index("blk")
    line = o * blk + z
    r = lax.rem(z, HEADS)
    z0 = z - r

    def at(index):
        return {"outer": index // blk, "blk": lax.rem(index, blk)}

    def mate(place):
        return {"outer": o, "blk": z0 + place}

    def partner(k):
        place = r
        if k % 2:
            place = place + 1 - 2 * lax.rem(place, 2)
        if k // 2:
            place = place + 2 - 4 * (place // 2)
        return place

    barrier = pltpu.get_barrier_semaphore()
    for k in range(1, HEADS):
        pl.semaphore_signal(
            barrier, inc=1, device_id=mate(partner(k)), device_id_type=MESH
        )
    for p in range(1, prior + 1):
        @pl.when(line >= HEADS * p)
        def _():
            pl.semaphore_signal(
                barrier, inc=1, device_id=at(line - HEADS * p), device_id_type=MESH
            )

        @pl.when(line + HEADS * p < total)
        def _():
            pl.semaphore_signal(
                barrier, inc=1, device_id=at(line + HEADS * p), device_id_type=MESH
            )

    def slab(place):
        return pl.ds(pl.multiple_of(place * rows, rows), rows)

    def cols(place):
        return pl.ds(pl.multiple_of(place * HEAD_DIM, HEAD_DIM), HEAD_DIM)

    def own_slab(place):
        return pl.ds(pl.multiple_of(own + place * rows, rows), rows)

    def routes(head, place):
        return (
            (kt_ref.at[:, cols(head)], ktb.at[own_slab(place), :]),
            (ks_ref.at[:, cols(head)], ksb.at[own_slab(place), :]),
            (qt_ref.at[:, cols(head)], qtb.at[slab(place), :]),
            (qs_ref.at[:, cols(head)], qsb.at[slab(place), :]),
            (pos_ref, posb.at[place]),
        )

    locals_ = [
        pltpu.make_async_copy(src, dst, local_sem.at[a])
        for a, (src, dst) in enumerate(routes(r, r))
    ]
    for copy in locals_:
        copy.start()

    for p in range(1, prior + 1):
        @pl.when(line < HEADS * p)
        def _():
            lo = (prior - p) * team_rows
            ktb[lo : lo + team_rows, :] = jnp.zeros((team_rows, HEAD_DIM), jnp.bfloat16)
            ksb[lo : lo + team_rows, :] = jnp.zeros((team_rows, HEAD_DIM), jnp.bfloat16)

    before = jnp.minimum(line // HEADS, prior)
    after = jnp.minimum((total - 1 - line) // HEADS, prior)
    pl.semaphore_wait(barrier, HEADS - 1 + before + after)

    def outgoing(k, a):
        place = partner(k)
        src, dst = routes(place, r)[a]
        return pltpu.make_async_remote_copy(
            src_ref=src, dst_ref=dst, send_sem=send_sem.at[k - 1, a], recv_sem=recv_sem.at[r, a],
            device_id=mate(place), device_id_type=MESH,
        )

    def incoming(k, a):
        place = partner(k)
        src, dst = routes(r, place)[a]
        return pltpu.make_async_remote_copy(
            src_ref=src, dst_ref=dst, send_sem=send_sem.at[k - 1, a],
            recv_sem=recv_sem.at[place, a],
            device_id=mate(place), device_id_type=MESH,
        )

    for group in ((0, 4, 2), (1,), (3,)):
        for a in group:
            for k in ORDER:
                outgoing(k, a).start()

    def forward(p, k, a, target):
        place = partner(k)
        buf = (ktb, ksb)[a]
        there = pl.ds(
            pl.multiple_of((prior - p) * team_rows + place * rows, rows), rows
        )
        return pltpu.make_async_remote_copy(
            src_ref=buf.at[own_slab(place), :], dst_ref=buf.at[there, :],
            send_sem=fsend.at[p - 1, place, a], recv_sem=frecv.at[p - 1, place, a],
            device_id=at(target), device_id_type=MESH,
        )

    def forward_all(k, a):
        for p in range(1, prior + 1):
            @pl.when(line + HEADS * p < total)
            def _():
                forward(p, k, a, line + HEADS * p).start()

    def forwarded(a):
        for p in range(1, prior + 1):
            @pl.when(line >= HEADS * p)
            def _():
                for k in range(HEADS):
                    forward(p, k, a, line - HEADS * p).wait_recv()

    def arrive(a):
        for k in ORDER:
            incoming(k, a).wait_recv()
            if a < 2:
                forward_all(k, a)

    for a in (0, 1):
        locals_[a].wait()
        forward_all(0, a)
    for a in (2, 3, 4):
        locals_[a].wait()
    arrive(0)
    arrive(4)
    arrive(2)
    forwarded(0)

    def send_part(block, target):
        p = prior - block // HEADS
        j = block % HEADS
        return pltpu.make_async_remote_copy(
            src_ref=part_out.at[block], dst_ref=part_in.at[p - 1, j],
            send_sem=psend.at[block], recv_sem=precv.at[p - 1, j],
            device_id=at(target), device_id_type=MESH,
        )

    def return_part(block):
        p = prior - block // HEADS

        @pl.when(line >= HEADS * p)
        def _():
            part_out[block] = acc[block * rows : (block + 1) * rows, :].astype(jnp.bfloat16)
            send_part(block, line - HEADS * p).start()

    def result(out, ref, send, recv, place, head):
        return pltpu.make_async_remote_copy(
            src_ref=out.at[place], dst_ref=ref.at[:, cols(head)],
            send_sem=send.at[place], recv_sem=recv.at[head],
            device_id=mate(place), device_id_type=MESH,
        )

    def give(i, value, ref, out, send, recv):
        @pl.when(r == i)
        def _():
            ref[:, cols(r)] = value.astype(jnp.bfloat16)

        @pl.when(r != i)
        def _():
            out[i] = value.astype(jnp.bfloat16)
            result(out, ref, send, recv, i, r).start()

    ahead = lax.broadcasted_iota(jnp.int32, (window, rows), 0) - lax.broadcasted_iota(
        jnp.int32, (window, rows), 1
    ) - own
    power = INV_ROOT * math.log2(math.e)

    def weights(keys, queries, seen):
        scores = lax.dot_general(
            keys, queries, (((1,), (1,)), ((), ())), preferred_element_type=jnp.float32
        )
        masked = jnp.where(seen, scores, LOWEST)
        top = jnp.max(masked, axis=0, keepdims=True)
        raised = jnp.exp2((masked - top) * power)
        return raised, LOSS_SCALE / jnp.sum(raised, axis=0, keepdims=True)

    def seen(i):
        return (ahead <= 0) & (ahead >= -posb[i])

    for i in range(HEADS):
        lo = i * rows
        raised, scale = weights(ktb[lo : lo + window, :], qtb[lo : lo + rows, :], seen(i))
        teacher[i] = raised * scale
    arrive(1)
    forwarded(1)
    arrive(3)

    for i in range(HEADS):
        lo = i * rows
        queries = qsb[lo : lo + rows, :]
        keys = ksb[lo : lo + window, :]
        raised, scale = weights(keys, queries, seen(i))
        grad = (raised * scale - teacher[i]).astype(jnp.bfloat16)
        dq = lax.dot_general(
            grad, keys, (((0,), (0,)), ((), ())), preferred_element_type=jnp.float32
        ) * INV_ROOT
        give(i, dq, dq_ref, dq_out, dqs, dqr)
        dk = jnp.dot(grad, queries, preferred_element_type=jnp.float32) * INV_ROOT
        if i == 0:
            acc[0:window, :] = dk
        else:
            acc[lo : lo + window - rows, :] += dk[: window - rows]
            acc[lo + window - rows : lo + window, :] = dk[window - rows :]
        return_part(i)
    for block in range(HEADS, blk):
        return_part(block)

    for j in range(HEADS):
        for p in range(1, prior + 1):
            @pl.when(line + HEADS * p < total)
            def _():
                send_part((prior - p) * HEADS + j, line + HEADS * p).wait_recv()
                lo = own + j * rows
                acc[lo : lo + rows, :] += part_in[p - 1, j].astype(jnp.float32)
        give(
            j, acc[own + j * rows : own + (j + 1) * rows, :], dk_ref, dk_out, dks, dkr
        )

    for k in ORDER:
        place = partner(k)
        result(dq_out, dq_ref, dqs, dqr, place, place).wait_recv()
        result(dk_out, dk_ref, dks, dkr, place, place).wait_recv()

    for k in range(1, HEADS):
        for a in range(5):
            outgoing(k, a).wait_send()
        place = partner(k)
        result(dq_out, dq_ref, dqs, dqr, place, r).wait_send()
        result(dk_out, dk_ref, dks, dkr, place, r).wait_send()
    for p in range(1, prior + 1):
        @pl.when(line + HEADS * p < total)
        def _():
            for k in range(HEADS):
                for a in range(2):
                    forward(p, k, a, line + HEADS * p).wait_send()

        @pl.when(line >= HEADS * p)
        def _():
            for j in range(HEADS):
                send_part((prior - p) * HEADS + j, line - HEADS * p).wait_send()


def body(q_teacher, k_teacher, q_student, k_student, positions):
    rows, width = q_teacher.shape
    blk = lax.axis_size("blk")
    total = lax.axis_size("outer") * blk
    prior = blk // HEADS
    span = (blk + HEADS) * rows
    bf16, f32 = jnp.bfloat16, jnp.float32
    tile = (rows, HEAD_DIM)
    dma = pltpu.SemaphoreType.DMA
    pairs = HEADS * (span * rows) * HEAD_DIM
    grads = pl.pallas_call(
        functools.partial(kernel, blk, total, rows),
        out_shape=[jax.ShapeDtypeStruct((rows, width), bf16)] * 2,
        in_specs=[pl.BlockSpec(memory_space=pltpu.HBM)] * 5,
        out_specs=[pl.BlockSpec(memory_space=pltpu.VMEM)] * 2,
        scratch_shapes=[
            pltpu.VMEM((span, HEAD_DIM), bf16),
            pltpu.VMEM((span, HEAD_DIM), bf16),
            pltpu.VMEM((HEADS * rows, HEAD_DIM), bf16),
            pltpu.VMEM((HEADS * rows, HEAD_DIM), bf16),
            pltpu.VMEM((HEADS, 1, rows), jnp.int32),
            pltpu.VMEM((HEADS, (blk + 1) * rows, rows), f32),
            pltpu.VMEM((span, HEAD_DIM), f32),
            pltpu.VMEM((HEADS,) + tile, bf16),
            pltpu.VMEM((HEADS,) + tile, bf16),
            pltpu.VMEM((blk,) + tile, bf16),
            pltpu.VMEM((prior, HEADS) + tile, bf16),
            dma((5,)),
            dma((HEADS - 1, 5)),
            dma((HEADS, 5)),
            dma((prior, HEADS, 2)),
            dma((prior, HEADS, 2)),
            dma((blk,)),
            dma((prior, HEADS)),
            dma((HEADS,)),
            dma((HEADS,)),
            dma((HEADS,)),
            dma((HEADS,)),
        ],
        compiler_params=pltpu.CompilerParams(
            collective_id=0, has_side_effects=True, vmem_limit_bytes=60 * 1024 * 1024
        ),
        cost_estimate=pl.CostEstimate(
            flops=8 * pairs, bytes_accessed=10 * rows * width * 2, transcendentals=2 * pairs // HEAD_DIM
        ),
    )(q_teacher, k_teacher, q_student, k_student, positions.reshape(1, rows))
    return tuple(grad.astype(f32) for grad in grads)


def solution(mesh):
    spec = P(("parts", "outer", "blk"), None)
    return jax.shard_map(
        body,
        mesh=mesh,
        in_specs=(spec, spec, spec, spec, P(("parts", "outer", "blk"))),
        out_specs=(spec, spec),
        check_vma=False,
    )
```

```python
import functools
import math

import jax
import jax.numpy as jnp
from jax import lax
from jax.experimental import pallas as pl
from jax.experimental.pallas import tpu as pltpu
from jax.sharding import PartitionSpec as P

HEADS = 4
HEAD_DIM = 128
LOSS_SCALE = 256
LOWEST = -1e30
INV_ROOT = HEAD_DIM ** (-0.5)
MESH = pl.DeviceIdType.MESH
ORDER = (3, 2, 1)


def kernel(
    blk, total, rows,
    qt_ref, kt_ref, qs_ref, ks_ref, pos_ref,
    dq_ref, dk_ref,
    ktb, ksb, qtb, qsb, posb,
    teacher, acc, dq_out, dk_out, part_out, part_in,
    local_sem, send_sem, recv_sem, fsend, frecv, psend, precv,
    dqs, dqr, dks, dkr,
):
    prior = blk // HEADS
    team_rows = HEADS * rows
    own = prior * team_rows
    window = own + rows
    o = lax.axis_index("outer")
    z = lax.axis_index("blk")
    line = o * blk + z
    r = lax.rem(z, HEADS)
    z0 = z - r

    def at(index):
        return {"outer": index // blk, "blk": lax.rem(index, blk)}

    def mate(place):
        return {"outer": o, "blk": z0 + place}

    def partner(k):
        place = r
        if k % 2:
            place = place + 1 - 2 * lax.rem(place, 2)
        if k // 2:
            place = place + 2 - 4 * (place // 2)
        return place

    barrier = pltpu.get_barrier_semaphore()
    for k in range(1, HEADS):
        pl.semaphore_signal(
            barrier, inc=1, device_id=mate(partner(k)), device_id_type=MESH
        )
    for p in range(1, prior + 1):
        @pl.when(line >= HEADS * p)
        def _():
            pl.semaphore_signal(
                barrier, inc=1, device_id=at(line - HEADS * p), device_id_type=MESH
            )

        @pl.when(line + HEADS * p < total)
        def _():
            pl.semaphore_signal(
                barrier, inc=1, device_id=at(line + HEADS * p), device_id_type=MESH
            )

    def slab(place):
        return pl.ds(pl.multiple_of(place * rows, rows), rows)

    def cols(place):
        return pl.ds(pl.multiple_of(place * HEAD_DIM, HEAD_DIM), HEAD_DIM)

    def own_slab(place):
        return pl.ds(pl.multiple_of(own + place * rows, rows), rows)

    def routes(head, place):
        return (
            (kt_ref.at[:, cols(head)], ktb.at[own_slab(place), :]),
            (ks_ref.at[:, cols(head)], ksb.at[own_slab(place), :]),
            (qt_ref.at[:, cols(head)], qtb.at[slab(place), :]),
            (qs_ref.at[:, cols(head)], qsb.at[slab(place), :]),
            (pos_ref, posb.at[place]),
        )

    locals_ = [
        pltpu.make_async_copy(src, dst, local_sem.at[a])
        for a, (src, dst) in enumerate(routes(r, r))
    ]
    for copy in locals_:
        copy.start()

    for p in range(1, prior + 1):
        @pl.when(line < HEADS * p)
        def _():
            lo = (prior - p) * team_rows
            ktb[lo : lo + team_rows, :] = jnp.zeros((team_rows, HEAD_DIM), jnp.bfloat16)
            ksb[lo : lo + team_rows, :] = jnp.zeros((team_rows, HEAD_DIM), jnp.bfloat16)

    before = jnp.minimum(line // HEADS, prior)
    after = jnp.minimum((total - 1 - line) // HEADS, prior)
    pl.semaphore_wait(barrier, HEADS - 1 + before + after)

    def outgoing(k, a):
        place = partner(k)
        src, dst = routes(place, r)[a]
        return pltpu.make_async_remote_copy(
            src_ref=src, dst_ref=dst, send_sem=send_sem.at[k - 1, a], recv_sem=recv_sem.at[r, a],
            device_id=mate(place), device_id_type=MESH,
        )

    def incoming(k, a):
        place = partner(k)
        src, dst = routes(r, place)[a]
        return pltpu.make_async_remote_copy(
            src_ref=src, dst_ref=dst, send_sem=send_sem.at[k - 1, a],
            recv_sem=recv_sem.at[place, a],
            device_id=mate(place), device_id_type=MESH,
        )

    for group in ((0, 4, 2), (1,), (3,)):
        for a in group:
            for k in ORDER:
                outgoing(k, a).start()

    def forward(p, k, a, target):
        place = partner(k)
        buf = (ktb, ksb)[a]
        there = pl.ds(
            pl.multiple_of((prior - p) * team_rows + place * rows, rows), rows
        )
        return pltpu.make_async_remote_copy(
            src_ref=buf.at[own_slab(place), :], dst_ref=buf.at[there, :],
            send_sem=fsend.at[p - 1, place, a], recv_sem=frecv.at[p - 1, place, a],
            device_id=at(target), device_id_type=MESH,
        )

    def forward_all(k, a):
        for p in range(1, prior + 1):
            @pl.when(line + HEADS * p < total)
            def _():
                forward(p, k, a, line + HEADS * p).start()

    def forwarded(a):
        for p in range(1, prior + 1):
            @pl.when(line >= HEADS * p)
            def _():
                for k in range(HEADS):
                    forward(p, k, a, line - HEADS * p).wait_recv()

    def arrive(a):
        for k in ORDER:
            incoming(k, a).wait_recv()
            if a < 2:
                forward_all(k, a)

    for a in (0, 1):
        locals_[a].wait()
        forward_all(0, a)
    for a in (2, 3, 4):
        locals_[a].wait()
    arrive(0)
    arrive(4)
    arrive(2)
    forwarded(0)

    def send_part(block, target):
        p = prior - block // HEADS
        j = block % HEADS
        return pltpu.make_async_remote_copy(
            src_ref=part_out.at[block], dst_ref=part_in.at[p - 1, j],
            send_sem=psend.at[block], recv_sem=precv.at[p - 1, j],
            device_id=at(target), device_id_type=MESH,
        )

    def return_part(block):
        p = prior - block // HEADS

        @pl.when(line >= HEADS * p)
        def _():
            part_out[block] = acc[block * rows : (block + 1) * rows, :].astype(jnp.bfloat16)
            send_part(block, line - HEADS * p).start()

    def result(out, ref, send, recv, place, head):
        return pltpu.make_async_remote_copy(
            src_ref=out.at[place], dst_ref=ref.at[:, cols(head)],
            send_sem=send.at[place], recv_sem=recv.at[head],
            device_id=mate(place), device_id_type=MESH,
        )

    def give(i, value, ref, out, send, recv):
        @pl.when(r == i)
        def _():
            ref[:, cols(r)] = value.astype(jnp.bfloat16)

        @pl.when(r != i)
        def _():
            out[i] = value.astype(jnp.bfloat16)
            result(out, ref, send, recv, i, r).start()

    ahead = lax.broadcasted_iota(jnp.int32, (window, rows), 0) - lax.broadcasted_iota(
        jnp.int32, (window, rows), 1
    ) - own
    power = INV_ROOT * math.log2(math.e)

    def weights(keys, queries, seen):
        scores = lax.dot_general(
            keys, queries, (((1,), (1,)), ((), ())), preferred_element_type=jnp.float32
        )
        masked = jnp.where(seen, scores, LOWEST)
        top = jnp.max(masked, axis=0, keepdims=True)
        raised = jnp.exp2((masked - top) * power)
        return raised, LOSS_SCALE / jnp.sum(raised, axis=0, keepdims=True)

    def seen(i):
        return (ahead <= 0) & (ahead >= -posb[i])

    for i in range(HEADS):
        lo = i * rows
        raised, scale = weights(ktb[lo : lo + window, :], qtb[lo : lo + rows, :], seen(i))
        teacher[i] = raised * scale
    arrive(1)
    forwarded(1)
    arrive(3)

    for i in range(HEADS):
        lo = i * rows
        queries = qsb[lo : lo + rows, :]
        keys = ksb[lo : lo + window, :]
        raised, scale = weights(keys, queries, seen(i))
        grad = (raised * scale - teacher[i]).astype(jnp.bfloat16)
        dq = lax.dot_general(
            grad, keys, (((0,), (0,)), ((), ())), preferred_element_type=jnp.float32
        ) * INV_ROOT
        give(i, dq, dq_ref, dq_out, dqs, dqr)
        dk = jnp.dot(grad, queries, preferred_element_type=jnp.float32) * INV_ROOT
        if i == 0:
            acc[0:window, :] = dk
        else:
            acc[lo : lo + window - rows, :] += dk[: window - rows]
            acc[lo + window - rows : lo + window, :] = dk[window - rows :]
        return_part(i)
    for block in range(HEADS, blk):
        return_part(block)

    for j in range(HEADS):
        for p in range(1, prior + 1):
            @pl.when(line + HEADS * p < total)
            def _():
                send_part((prior - p) * HEADS + j, line + HEADS * p).wait_recv()
                lo = own + j * rows
                acc[lo : lo + rows, :] += part_in[p - 1, j].astype(jnp.float32)
        give(
            j, acc[own + j * rows : own + (j + 1) * rows, :], dk_ref, dk_out, dks, dkr
        )

    for k in ORDER:
        place = partner(k)
        result(dq_out, dq_ref, dqs, dqr, place, place).wait_recv()
        result(dk_out, dk_ref, dks, dkr, place, place).wait_recv()

    for k in range(1, HEADS):
        for a in range(5):
            outgoing(k, a).wait_send()
        place = partner(k)
        result(dq_out, dq_ref, dqs, dqr, place, r).wait_send()
        result(dk_out, dk_ref, dks, dkr, place, r).wait_send()
    for p in range(1, prior + 1):
        @pl.when(line + HEADS * p < total)
        def _():
            for k in range(HEADS):
                for a in range(2):
                    forward(p, k, a, line + HEADS * p).wait_send()

        @pl.when(line >= HEADS * p)
        def _():
            for j in range(HEADS):
                send_part((prior - p) * HEADS + j, line - HEADS * p).wait_send()


def widen(dq_ref, dk_ref, dq_wide, dk_wide):
    dq_wide[...] = dq_ref[...].astype(jnp.float32)
    dk_wide[...] = dk_ref[...].astype(jnp.float32)


def body(q_teacher, k_teacher, q_student, k_student, positions):
    rows, width = q_teacher.shape
    blk = lax.axis_size("blk")
    total = lax.axis_size("outer") * blk
    prior = blk // HEADS
    span = (blk + HEADS) * rows
    bf16, f32 = jnp.bfloat16, jnp.float32
    tile = (rows, HEAD_DIM)
    dma = pltpu.SemaphoreType.DMA
    pairs = HEADS * (span * rows) * HEAD_DIM
    grads = pl.pallas_call(
        functools.partial(kernel, blk, total, rows),
        out_shape=[jax.ShapeDtypeStruct((rows, width), bf16)] * 2,
        in_specs=[pl.BlockSpec(memory_space=pltpu.HBM)] * 5,
        out_specs=[pl.BlockSpec(memory_space=pltpu.VMEM)] * 2,
        scratch_shapes=[
            pltpu.VMEM((span, HEAD_DIM), bf16),
            pltpu.VMEM((span, HEAD_DIM), bf16),
            pltpu.VMEM((HEADS * rows, HEAD_DIM), bf16),
            pltpu.VMEM((HEADS * rows, HEAD_DIM), bf16),
            pltpu.VMEM((HEADS, 1, rows), jnp.int32),
            pltpu.VMEM((HEADS, (blk + 1) * rows, rows), f32),
            pltpu.VMEM((span, HEAD_DIM), f32),
            pltpu.VMEM((HEADS,) + tile, bf16),
            pltpu.VMEM((HEADS,) + tile, bf16),
            pltpu.VMEM((blk,) + tile, bf16),
            pltpu.VMEM((prior, HEADS) + tile, bf16),
            dma((5,)),
            dma((HEADS - 1, 5)),
            dma((HEADS, 5)),
            dma((prior, HEADS, 2)),
            dma((prior, HEADS, 2)),
            dma((blk,)),
            dma((prior, HEADS)),
            dma((HEADS,)),
            dma((HEADS,)),
            dma((HEADS,)),
            dma((HEADS,)),
        ],
        compiler_params=pltpu.CompilerParams(
            collective_id=0, has_side_effects=True, vmem_limit_bytes=60 * 1024 * 1024
        ),
        cost_estimate=pl.CostEstimate(
            flops=8 * pairs, bytes_accessed=10 * rows * width * 2, transcendentals=2 * pairs // HEAD_DIM
        ),
    )(q_teacher, k_teacher, q_student, k_student, positions.reshape(1, rows))
    return pl.pallas_call(
        widen,
        out_shape=[jax.ShapeDtypeStruct((rows, width), f32)] * 2,
        in_specs=[pl.BlockSpec(memory_space=pltpu.VMEM)] * 2,
        out_specs=[pl.BlockSpec(memory_space=pltpu.VMEM)] * 2,
    )(*grads)


def solution(mesh):
    spec = P(("parts", "outer", "blk"), None)
    return jax.shard_map(
        body,
        mesh=mesh,
        in_specs=(spec, spec, spec, spec, P(("parts", "outer", "blk"))),
        out_specs=(spec, spec),
        check_vma=False,
    )
```

```python
import functools
import math

import jax
import jax.numpy as jnp
from jax import lax
from jax.experimental import pallas as pl
from jax.experimental.pallas import tpu as pltpu
from jax.sharding import PartitionSpec as P

HEADS = 4
HEAD_DIM = 128
LOSS_SCALE = 256
LOWEST = -1e30
INV_ROOT = HEAD_DIM ** (-0.5)
MESH = pl.DeviceIdType.MESH
ORDER = (3, 2, 1)


def kernel(
    blk, total, rows,
    qt_ref, kt_ref, qs_ref, ks_ref, pos_ref,
    dq_ref, dk_ref,
    ktb, ksb, qtb, qsb, posb,
    teacher, acc, dq_out, dk_out, part_out, part_in,
    local_sem, send_sem, recv_sem, fsend, frecv, psend, precv,
    dqs, dqr, dks, dkr,
):
    prior = blk // HEADS
    team_rows = HEADS * rows
    own = prior * team_rows
    window = own + rows
    o = lax.axis_index("outer")
    z = lax.axis_index("blk")
    line = o * blk + z
    r = lax.rem(z, HEADS)
    z0 = z - r

    def at(index):
        return {"outer": index // blk, "blk": lax.rem(index, blk)}

    def mate(place):
        return {"outer": o, "blk": z0 + place}

    def partner(k):
        place = r
        if k % 2:
            place = place + 1 - 2 * lax.rem(place, 2)
        if k // 2:
            place = place + 2 - 4 * (place // 2)
        return place

    barrier = pltpu.get_barrier_semaphore()
    for k in range(1, HEADS):
        pl.semaphore_signal(
            barrier, inc=1, device_id=mate(partner(k)), device_id_type=MESH
        )
    for p in range(1, prior + 1):
        @pl.when(line >= HEADS * p)
        def _():
            pl.semaphore_signal(
                barrier, inc=1, device_id=at(line - HEADS * p), device_id_type=MESH
            )

        @pl.when(line + HEADS * p < total)
        def _():
            pl.semaphore_signal(
                barrier, inc=1, device_id=at(line + HEADS * p), device_id_type=MESH
            )

    def slab(place):
        return pl.ds(pl.multiple_of(place * rows, rows), rows)

    def cols(place):
        return pl.ds(pl.multiple_of(place * HEAD_DIM, HEAD_DIM), HEAD_DIM)

    def own_slab(place):
        return pl.ds(pl.multiple_of(own + place * rows, rows), rows)

    def routes(head, place):
        return (
            (kt_ref.at[:, cols(head)], ktb.at[own_slab(place), :]),
            (ks_ref.at[:, cols(head)], ksb.at[own_slab(place), :]),
            (qt_ref.at[:, cols(head)], qtb.at[slab(place), :]),
            (qs_ref.at[:, cols(head)], qsb.at[slab(place), :]),
            (pos_ref, posb.at[place]),
        )

    locals_ = [
        pltpu.make_async_copy(src, dst, local_sem.at[a])
        for a, (src, dst) in enumerate(routes(r, r))
    ]
    for copy in locals_:
        copy.start()

    for p in range(1, prior + 1):
        @pl.when(line < HEADS * p)
        def _():
            lo = (prior - p) * team_rows
            ktb[lo : lo + team_rows, :] = jnp.zeros((team_rows, HEAD_DIM), jnp.bfloat16)
            ksb[lo : lo + team_rows, :] = jnp.zeros((team_rows, HEAD_DIM), jnp.bfloat16)

    before = jnp.minimum(line // HEADS, prior)
    after = jnp.minimum((total - 1 - line) // HEADS, prior)
    pl.semaphore_wait(barrier, HEADS - 1 + before + after)

    def outgoing(k, a):
        place = partner(k)
        src, dst = routes(place, r)[a]
        return pltpu.make_async_remote_copy(
            src_ref=src, dst_ref=dst, send_sem=send_sem.at[k - 1, a], recv_sem=recv_sem.at[r, a],
            device_id=mate(place), device_id_type=MESH,
        )

    def incoming(k, a):
        place = partner(k)
        src, dst = routes(r, place)[a]
        return pltpu.make_async_remote_copy(
            src_ref=src, dst_ref=dst, send_sem=send_sem.at[k - 1, a],
            recv_sem=recv_sem.at[place, a],
            device_id=mate(place), device_id_type=MESH,
        )

    for group in ((0, 4, 2), (1,), (3,)):
        for a in group:
            for k in ORDER:
                outgoing(k, a).start()

    def forward(p, k, a, target):
        place = partner(k)
        buf = (ktb, ksb)[a]
        there = pl.ds(
            pl.multiple_of((prior - p) * team_rows + place * rows, rows), rows
        )
        return pltpu.make_async_remote_copy(
            src_ref=buf.at[own_slab(place), :], dst_ref=buf.at[there, :],
            send_sem=fsend.at[p - 1, place, a], recv_sem=frecv.at[p - 1, place, a],
            device_id=at(target), device_id_type=MESH,
        )

    def forward_all(k, a):
        for p in range(1, prior + 1):
            @pl.when(line + HEADS * p < total)
            def _():
                forward(p, k, a, line + HEADS * p).start()

    def forwarded(a):
        for p in range(1, prior + 1):
            @pl.when(line >= HEADS * p)
            def _():
                for k in range(HEADS):
                    forward(p, k, a, line - HEADS * p).wait_recv()

    def arrive(a):
        for k in ORDER:
            incoming(k, a).wait_recv()
            if a < 2:
                forward_all(k, a)

    for a in (0, 1):
        locals_[a].wait()
        forward_all(0, a)
    for a in (2, 3, 4):
        locals_[a].wait()
    arrive(0)
    arrive(4)
    arrive(2)
    forwarded(0)

    def send_part(block, target):
        p = prior - block // HEADS
        j = block % HEADS
        return pltpu.make_async_remote_copy(
            src_ref=part_out.at[block], dst_ref=part_in.at[p - 1, j],
            send_sem=psend.at[block], recv_sem=precv.at[p - 1, j],
            device_id=at(target), device_id_type=MESH,
        )

    def return_part(block):
        p = prior - block // HEADS

        @pl.when(line >= HEADS * p)
        def _():
            part_out[block] = acc[block * rows : (block + 1) * rows, :].astype(jnp.bfloat16)
            send_part(block, line - HEADS * p).start()

    def result(out, ref, send, recv, place, head):
        return pltpu.make_async_remote_copy(
            src_ref=out.at[place], dst_ref=ref.at[:, cols(head)],
            send_sem=send.at[place], recv_sem=recv.at[head],
            device_id=mate(place), device_id_type=MESH,
        )

    def give(i, value, ref, out, send, recv):
        @pl.when(r == i)
        def _():
            ref[:, cols(r)] = value.astype(jnp.bfloat16)

        @pl.when(r != i)
        def _():
            out[i] = value.astype(jnp.bfloat16)
            result(out, ref, send, recv, i, r).start()

    ahead = lax.broadcasted_iota(jnp.int32, (window, rows), 0) - lax.broadcasted_iota(
        jnp.int32, (window, rows), 1
    ) - own
    power = INV_ROOT * math.log2(math.e)

    def weights(keys, queries, seen):
        scores = lax.dot_general(
            keys, queries, (((1,), (1,)), ((), ())), preferred_element_type=jnp.float32
        )
        masked = jnp.where(seen, scores, LOWEST)
        top = jnp.max(masked, axis=0, keepdims=True)
        raised = jnp.exp2((masked - top) * power)
        return raised, LOSS_SCALE / jnp.sum(raised, axis=0, keepdims=True)

    def seen(i):
        return (ahead <= 0) & (ahead >= -posb[i])

    for i in range(HEADS):
        lo = i * rows
        raised, scale = weights(ktb[lo : lo + window, :], qtb[lo : lo + rows, :], seen(i))
        teacher[i] = raised * scale
    arrive(1)
    forwarded(1)

    for i in range(HEADS):
        lo = i * rows

        @pl.when(r != i)
        def _():
            src, dst = routes(r, i)[3]
            pltpu.make_async_remote_copy(
                src_ref=src, dst_ref=dst, send_sem=send_sem.at[0, 3], recv_sem=recv_sem.at[i, 3],
                device_id=mate(i), device_id_type=MESH,
            ).wait_recv()

        queries = qsb[lo : lo + rows, :]
        keys = ksb[lo : lo + window, :]
        raised, scale = weights(keys, queries, seen(i))
        grad = (raised * scale - teacher[i]).astype(jnp.bfloat16)
        dq = lax.dot_general(
            grad, keys, (((0,), (0,)), ((), ())), preferred_element_type=jnp.float32
        ) * INV_ROOT
        give(i, dq, dq_ref, dq_out, dqs, dqr)
        dk = jnp.dot(grad, queries, preferred_element_type=jnp.float32) * INV_ROOT
        if i == 0:
            acc[0:window, :] = dk
        else:
            acc[lo : lo + window - rows, :] += dk[: window - rows]
            acc[lo + window - rows : lo + window, :] = dk[window - rows :]
        return_part(i)
    for block in range(HEADS, blk):
        return_part(block)

    for j in range(HEADS):
        for p in range(1, prior + 1):
            @pl.when(line + HEADS * p < total)
            def _():
                send_part((prior - p) * HEADS + j, line + HEADS * p).wait_recv()
                lo = own + j * rows
                acc[lo : lo + rows, :] += part_in[p - 1, j].astype(jnp.float32)
        give(
            j, acc[own + j * rows : own + (j + 1) * rows, :], dk_ref, dk_out, dks, dkr
        )

    for k in ORDER:
        place = partner(k)
        result(dq_out, dq_ref, dqs, dqr, place, place).wait_recv()
        result(dk_out, dk_ref, dks, dkr, place, place).wait_recv()

    for k in range(1, HEADS):
        for a in range(5):
            outgoing(k, a).wait_send()
        place = partner(k)
        result(dq_out, dq_ref, dqs, dqr, place, r).wait_send()
        result(dk_out, dk_ref, dks, dkr, place, r).wait_send()
    for p in range(1, prior + 1):
        @pl.when(line + HEADS * p < total)
        def _():
            for k in range(HEADS):
                for a in range(2):
                    forward(p, k, a, line + HEADS * p).wait_send()

        @pl.when(line >= HEADS * p)
        def _():
            for j in range(HEADS):
                send_part((prior - p) * HEADS + j, line - HEADS * p).wait_send()


def widen(dq_ref, dk_ref, dq_wide, dk_wide):
    dq_wide[...] = dq_ref[...].astype(jnp.float32)
    dk_wide[...] = dk_ref[...].astype(jnp.float32)


def body(q_teacher, k_teacher, q_student, k_student, positions):
    rows, width = q_teacher.shape
    blk = lax.axis_size("blk")
    total = lax.axis_size("outer") * blk
    prior = blk // HEADS
    span = (blk + HEADS) * rows
    bf16, f32 = jnp.bfloat16, jnp.float32
    tile = (rows, HEAD_DIM)
    dma = pltpu.SemaphoreType.DMA
    pairs = HEADS * (span * rows) * HEAD_DIM
    grads = pl.pallas_call(
        functools.partial(kernel, blk, total, rows),
        out_shape=[jax.ShapeDtypeStruct((rows, width), bf16)] * 2,
        in_specs=[pl.BlockSpec(memory_space=pltpu.HBM)] * 5,
        out_specs=[pl.BlockSpec(memory_space=pltpu.VMEM)] * 2,
        scratch_shapes=[
            pltpu.VMEM((span, HEAD_DIM), bf16),
            pltpu.VMEM((span, HEAD_DIM), bf16),
            pltpu.VMEM((HEADS * rows, HEAD_DIM), bf16),
            pltpu.VMEM((HEADS * rows, HEAD_DIM), bf16),
            pltpu.VMEM((HEADS, 1, rows), jnp.int32),
            pltpu.VMEM((HEADS, (blk + 1) * rows, rows), f32),
            pltpu.VMEM((span, HEAD_DIM), f32),
            pltpu.VMEM((HEADS,) + tile, bf16),
            pltpu.VMEM((HEADS,) + tile, bf16),
            pltpu.VMEM((blk,) + tile, bf16),
            pltpu.VMEM((prior, HEADS) + tile, bf16),
            dma((5,)),
            dma((HEADS - 1, 5)),
            dma((HEADS, 5)),
            dma((prior, HEADS, 2)),
            dma((prior, HEADS, 2)),
            dma((blk,)),
            dma((prior, HEADS)),
            dma((HEADS,)),
            dma((HEADS,)),
            dma((HEADS,)),
            dma((HEADS,)),
        ],
        compiler_params=pltpu.CompilerParams(
            collective_id=0, has_side_effects=True, vmem_limit_bytes=60 * 1024 * 1024
        ),
        cost_estimate=pl.CostEstimate(
            flops=8 * pairs, bytes_accessed=10 * rows * width * 2, transcendentals=2 * pairs // HEAD_DIM
        ),
    )(q_teacher, k_teacher, q_student, k_student, positions.reshape(1, rows))
    return pl.pallas_call(
        widen,
        out_shape=[jax.ShapeDtypeStruct((rows, width), f32)] * 2,
        in_specs=[pl.BlockSpec(memory_space=pltpu.VMEM)] * 2,
        out_specs=[pl.BlockSpec(memory_space=pltpu.VMEM)] * 2,
    )(*grads)


def solution(mesh):
    spec = P(("parts", "outer", "blk"), None)
    return jax.shard_map(
        body,
        mesh=mesh,
        in_specs=(spec, spec, spec, spec, P(("parts", "outer", "blk"))),
        out_specs=(spec, spec),
        check_vma=False,
    )
```
